256 devices in a mesh: dom: 64 (over z, x, core), rep: 4 (over y).
Axes of the slice: x: 4, y: 4, z: 8, core: 2. Of those that a mesh axis runs over, the one named last changes fastest.
Arguments:
- features: bfloat16 [262144, 256], P(('dom', 'rep')), may hold values from -6 to 6
- history: bfloat16 [4, 262144, 256], P(None, 'dom'), may hold values from -6 to 6
- tiles: bfloat16 [8192, 128, 128], P(('dom', 'rep')), may hold values from -0.25 to 0.25
- tile_cols: int32 [8192], P(('dom', 'rep')), may hold values from 0 to 7
- halo_ids: int32 [4, 393216], P(None, ('dom', 'rep')), may hold values from 0 to 4095
- halo_counts: int32 [4, 16384], P(None, ('dom', 'rep')), may hold values from 1 to 24, as said below
- halo_dst: int32 [4, 393216], P(None, ('dom', 'rep')), may hold values from 0 to 1023
- halo_wt: bfloat16 [4, 393216], P(None, ('dom', 'rep')), may hold values from 0.25 to 1
- weights: bfloat16 [4, 256, 256], replicated, may hold values from -0.375 to 0.375
- cotangent: bfloat16 [262144, 256], P(('dom', 'rep')), may hold values from -0.03125 to 0.03125
Outputs:
- embeddings: bfloat16 [262144, 256], P(('dom', 'rep'))
- new_history: bfloat16 [3, 262144, 256], P(None, 'dom')
- weight_grad: float32 [4, 256, 256], replicated
The draws below stay inside these ranges and needn't reach their ends.
Inputs may be any that keep to these rules, and one draw needn't show every extreme that they name: `halo_counts`: in every layer, every device has some owner with 24 live slots, and some owner receives 24 live slots from every device; the other counts are independent. Slots past the count hold valid but unused ids.
All inputs are finite; a program needn't handle non-finite values.
Results may differ from the reference program's by a relative error of at most 0.02.
Values may be sent and summed in bfloat16 or wider, within the bound.
No kernel may reach another device: no remote copies, remote signals or barrier semaphores. Data moves between devices by JAX's collectives and lax.ppermute only.
A program may use at most 128 MiB of HBM per device.

```python
import jax
import jax.numpy as jnp
from jax import lax

H = 256
LAYERS = 4
ROWS = 1024
CAP = 24
TPR = 4
PARTS_SIZE = 64
REPLICAS = 4
NB = 8
SLAB = 4096
SLOTS = 1536
ROWS_TOT = 262144
TILES = 8192


def draw_halo_counts(key, part):
    key = jax.random.fold_in(key, 7)
    base_key, full_key = jax.random.split(key)
    devices = PARTS_SIZE * REPLICAS
    base = jax.random.randint(base_key, (LAYERS, devices, PARTS_SIZE), 1, CAP + 1)
    chosen = jax.random.randint(full_key, (LAYERS, 1, 1), 0, PARTS_SIZE)
    owner = jnp.arange(PARTS_SIZE, dtype=jnp.int32)[None, None, :]
    counts = jnp.where(owner == chosen, CAP, base)
    return counts.reshape(LAYERS, devices * PARTS_SIZE).astype(jnp.int32)


def place_ends(array, key, smallest, largest):
    extent = array.shape
    index_at = [jax.random.randint(jax.random.fold_in(key, axis), (), 0, extent[axis]) for axis in range(len(extent))]
    array = array.at[tuple(index_at)].set(smallest)
    longest = extent.index(max(extent))
    index_at[longest] = (index_at[longest] + 1) % extent[longest]
    return array.at[tuple(index_at)].set(largest)


def block_levels(rng, extent, cuts, smallest, top_value):
    factor_of, own = 1.0, jax.random.fold_in(rng, 6)
    for dim, parts in cuts:
        steps = jnp.exp(jax.random.uniform(jax.random.fold_in(own, dim), (parts,), jnp.float32, smallest / len(cuts), top_value / len(cuts)))
        factor_of = factor_of * jnp.repeat(steps, extent[dim] // parts).reshape([-1 if axis == dim else 1 for axis in range(len(extent))])
    return factor_of


def scatter_about(stream_key, extent, scale, most, shards=(), held_as=jnp.bfloat16):
    result = jax.random.normal(stream_key, extent, jnp.float32) * scale
    if len(shards) > 0:
        result = block_levels(stream_key, extent, shards, -0.22, 0.18) * result
    return jnp.clip(result, min=-most, max=most).astype(held_as)


def setup_inputs(seed: int = 0) -> dict:
    keys = jax.random.split(jax.random.key(seed), 11)
    return {
        "features": scatter_about(keys[0], (ROWS_TOT, H), 1.0, 6.0, ((0, 256),)),
        "history": scatter_about(keys[1], (LAYERS, ROWS_TOT, H), 1.0, 6.0, ((1, 64),)),
        "tiles": scatter_about(keys[2], (TILES, 128, 128), (TPR * 128) ** -0.5, 0.25, ((0, 256),)),
        "tile_cols": place_ends(jax.random.randint(keys[3], (TILES,), 0, NB), jax.random.fold_in(keys[3], 1), 0, NB - 1).astype(jnp.int32),
        "halo_ids": place_ends(jax.random.randint(keys[4], (LAYERS, ROWS_TOT // ROWS * SLOTS), 0, SLAB), jax.random.fold_in(keys[4], 1), 0, SLAB - 1).astype(jnp.int32),
        "halo_counts": draw_halo_counts(jax.random.fold_in(keys[10], 71), 0),
        "halo_dst": place_ends(jax.random.randint(keys[6], (LAYERS, ROWS_TOT // ROWS * SLOTS), 0, ROWS), jax.random.fold_in(keys[6], 1), 0, ROWS - 1).astype(jnp.int32),
        "halo_wt": jnp.clip(0.25 + 0.75 * jax.random.uniform(keys[7], (LAYERS, ROWS_TOT // ROWS * SLOTS), jnp.float32) ** block_levels(keys[7], (LAYERS, ROWS_TOT // ROWS * SLOTS), ((1, 256),), -0.2, 0.2), 0.25, 1.0).astype(jnp.bfloat16),
        "weights": scatter_about(keys[8], (LAYERS, H, H), H ** -0.5, 0.375),
        "cotangent": scatter_about(keys[9], (ROWS_TOT, H), (ROWS_TOT ** -0.5), 0.03125, ((0, 256),)),
    }


restart_rate = 0.1

def block_sum(tile_part, col_part, hidden):
    blocks = hidden.reshape(NB, 128, H)
    gathered = blocks[col_part]
    product = jnp.einsum('tij,tjw->tiw', tile_part.astype(jnp.float32), gathered.astype(jnp.float32))
    return product.reshape(NB, TPR, 128, H).sum(axis=1).reshape(ROWS, H)

def block_back(tile_part, col_part, grad_bf):
    blocks = grad_bf.reshape(NB, 128, H)
    spread = jnp.broadcast_to(blocks[:, None], (NB, TPR, 128, H)).reshape(NB * TPR, 128, H)
    product = jnp.einsum('tji,tjw->tiw', tile_part.astype(jnp.float32), spread.astype(jnp.float32))
    select = (col_part[:, None] == jnp.arange(NB, dtype=jnp.int32)[None, :]).astype(jnp.float32)
    return jnp.einsum('tn,tiw->niw', select, product, precision=lax.Precision.HIGHEST).reshape(ROWS, H)

def reference(features, history, tiles, tile_cols, halo_ids, halo_counts, halo_dst, halo_wt, weights, cotangent):
    devices = PARTS_SIZE * REPLICAS
    tiles_dev = tiles.reshape(devices, NB * TPR, 128, 128)
    cols_dev = tile_cols.reshape(devices, NB * TPR)

    def forward_tiles(hidden):
        return lax.map(lambda packed: block_sum(packed[0], packed[1], packed[2]), (tiles_dev, cols_dev, hidden.reshape(devices, ROWS, H))).reshape(ROWS_TOT, H)

    def backward_tiles(grad_bf):
        return lax.map(lambda packed: block_back(packed[0], packed[1], packed[2]), (tiles_dev, cols_dev, grad_bf.reshape(devices, ROWS, H))).reshape(ROWS_TOT, H)
    owner = jnp.arange(PARTS_SIZE, dtype=jnp.int32)[None, :, None]
    slot_rank = jnp.arange(CAP, dtype=jnp.int32)
    device_base = jnp.arange(devices, dtype=jnp.int32)[:, None] * ROWS
    hidden = features
    saved = []
    fresh = []
    for depth in range(LAYERS):
        beta = math_log(depth)
        slot_ids = halo_ids[depth].reshape(devices, PARTS_SIZE, CAP).astype(jnp.int32)
        source_rows = (owner * SLAB + slot_ids).reshape(-1).astype(jnp.int32)
        pulled = jnp.take(history[depth], source_rows, axis=0)
        live = (slot_rank[None, None, :] < halo_counts[depth].reshape(devices, PARTS_SIZE)[:, :, None]).reshape(-1)
        slot_weight = jnp.where(live, halo_wt[depth].astype(jnp.float32), jnp.zeros((), jnp.float32))
        target = (device_base + halo_dst[depth].reshape(devices, SLOTS)).reshape(-1).astype(jnp.int32)
        halo_term = jax.ops.segment_sum(pulled.astype(jnp.float32) * slot_weight[:, None], target, num_segments=ROWS_TOT)
        support = (1.0 - restart_rate) * (forward_tiles(hidden) + halo_term) + restart_rate * features.astype(jnp.float32)
        support_bf = support.astype(jnp.bfloat16)
        preact = (1.0 - beta) * support + beta * jnp.dot(support_bf, weights[depth], preferred_element_type=jnp.float32)
        saved.append((support_bf, preact))
        hidden = jax.nn.gelu(preact).astype(jnp.bfloat16)
        if depth + 1 < LAYERS:
            fresh.append(hidden)
    grad_out = cotangent
    partial_value = []
    for depth in range(LAYERS - 1, -1, -1):
        beta = math_log(depth)
        support_bf, preact = saved[depth]
        gelu_grad = jax.vjp(jax.nn.gelu, preact)[1](grad_out.astype(jnp.float32))[0]
        grad_bf = gelu_grad.astype(jnp.bfloat16)
        partial_value.append(beta * lax.dot_general(support_bf, grad_bf, (((0,), (0,)), ((), ())), preferred_element_type=jnp.float32))
        if depth > 0:
            grad_support = (1.0 - beta) * gelu_grad + beta * jnp.dot(grad_bf, weights[depth].T, preferred_element_type=jnp.float32)
            grad_out = ((1.0 - restart_rate) * backward_tiles(grad_support.astype(jnp.bfloat16))).astype(jnp.bfloat16)
    weight_grad = jnp.stack(partial_value[::-1])
    return (hidden, jnp.stack(fresh), weight_grad)

def math_log(depth):
    return float(jnp.log(0.5 / (depth + 1) + 1.0)) if False else _beta_table(depth)

def _beta_table(depth):
    import_free = [0.4054651081081644, 0.22314355131420976, 0.15415067982725836, 0.11778303565638346, 0.09531017980432493, 0.08004270767353637, 0.06899287148695142, 0.06062462181643484]
    return import_free[depth]
```

```python
import functools

import jax
import jax.numpy as jnp
from jax import lax
from jax.experimental import pallas as pl
from jax.experimental.pallas import tpu as pltpu
from jax.sharding import PartitionSpec as P

restart_rate = 0.1
beta_table = [
    0.4054651081081644,
    0.22314355131420976,
    0.15415067982725836,
    0.11778303565638346,
    0.09531017980432493,
    0.08004270767353637,
    0.06899287148695142,
    0.06062462181643484,
]
f32 = jnp.float32
bf16 = jnp.bfloat16
gelu_c = 0.7978845608028654
gelu_k = 0.044715
vmem_limit = 40 * 1024 * 1024
VMEM = pl.BlockSpec(memory_space=pltpu.VMEM)
SMEM = pl.BlockSpec(memory_space=pltpu.SMEM)
ANY = pl.BlockSpec(memory_space=pl.ANY)


def forward_kernel(beta, cols, hidden, tiles, pulled, dst, wt, features, weight, support_o, slope_o, hidden_o):
    slots = pulled.shape[0]
    row_count = features.shape[0]
    step = 256
    per_block = tiles.shape[0] // (row_count // 128)
    dst_row = dst[...]
    wt_row = wt[...]
    for chunk in range(row_count // step):
        lo = chunk * step
        position = lax.broadcasted_iota(jnp.int32, (step, slots), 0) + lo
        scatter = jnp.where(dst_row == position, wt_row, 0.0).astype(bf16)
        acc = jnp.dot(scatter, pulled[...], preferred_element_type=f32)
        parts = []
        for block in range(lo // 128, (lo + step) // 128):
            picked = jnp.concatenate(
                [
                    hidden[pl.ds(pl.multiple_of(cols[block * per_block + k] * 128, 128), 128), :]
                    for k in range(per_block)
                ],
                axis=0,
            )
            tile_row = jnp.concatenate([tiles[block * per_block + k] for k in range(per_block)], axis=1)
            parts.append(jnp.dot(tile_row, picked, preferred_element_type=f32))
        acc = acc + jnp.concatenate(parts, axis=0)
        support = (1.0 - restart_rate) * acc + restart_rate * features[lo : lo + step, :].astype(f32)
        support_bf = support.astype(bf16)
        support_o[lo : lo + step, :] = support_bf
        pre = (1.0 - beta) * support + beta * jnp.dot(support_bf, weight[...], preferred_element_type=f32)
        square = pre * pre
        th = jnp.tanh(gelu_c * (pre + gelu_k * pre * square))
        half = 0.5 * (1.0 + th)
        hidden_o[lo : lo + step, :] = (pre * half).astype(bf16)
        slope_o[lo : lo + step, :] = half + 0.5 * pre * (1.0 - th * th) * (
            gelu_c * (1.0 + 3.0 * gelu_k * square)
        )


def forward_layer(beta, cols, hidden, tiles, pulled, dst, wt, features, weight):
    rows, width = features.shape
    return pl.pallas_call(
        functools.partial(forward_kernel, beta),
        out_shape=(
            jax.ShapeDtypeStruct((rows, width), bf16),
            jax.ShapeDtypeStruct((rows, width), f32),
            jax.ShapeDtypeStruct((rows, width), bf16),
        ),
        in_specs=[SMEM] + [VMEM] * 7,
        out_specs=(VMEM, VMEM, VMEM),
        compiler_params=pltpu.CompilerParams(vmem_limit_bytes=vmem_limit),
        cost_estimate=pl.CostEstimate(flops=1_300_000_000, bytes_accessed=6_000_000, transcendentals=262144),
    )(cols, hidden, tiles, pulled, dst, wt, features, weight)


def backward_kernel(cols, cot, tiles_t, weights, *rest):
    layer_count = weights.shape[0]
    supports = rest[:layer_count]
    slopes = rest[layer_count : 2 * layer_count]
    grads_o, total, grad_bf, gs_bf = rest[2 * layer_count :]
    row_count, width = cot.shape
    step = 256
    per_block = tiles_t.shape[0] // (row_count // 128)
    for depth in range(layer_count - 1, -1, -1):
        beta = beta_table[depth]
        weight = weights[depth]
        for chunk in range(row_count // step):
            lo = chunk * step
            if depth == layer_count - 1:
                grad_out = cot[lo : lo + step, :].astype(f32)
            else:
                grad_out = ((1.0 - restart_rate) * total[lo : lo + step, :]).astype(bf16).astype(f32)
            gp = grad_out * slopes[depth][lo : lo + step, :]
            gp_bf = gp.astype(bf16)
            grad_bf[lo : lo + step, :] = gp_bf
            if depth > 0:
                gs = (1.0 - beta) * gp + beta * lax.dot_general(
                    gp_bf, weight, (((1,), (1,)), ((), ())), preferred_element_type=f32
                )
                gs_bf[lo : lo + step, :] = gs.astype(bf16)
        grads_o[depth] = (
            beta
            * lax.dot_general(
                supports[depth][...], grad_bf[...], (((0,), (0,)), ((), ())), preferred_element_type=f32
            )
        ).astype(bf16)
        if depth > 0:
            total[...] = jnp.zeros_like(total)
            for block in range(row_count // 128):
                tile_col = jnp.concatenate(
                    [tiles_t[block * per_block + k] for k in range(per_block)], axis=0
                )
                product = jnp.dot(
                    tile_col, gs_bf[block * 128 : (block + 1) * 128, :], preferred_element_type=f32
                )
                for k in range(per_block):
                    at = pl.ds(pl.multiple_of(cols[block * per_block + k] * 128, 128), 128)
                    total[at, :] = total[at, :] + product[k * 128 : (k + 1) * 128, :]


def backward(cols, cot, tiles_t, weights, supports, slopes):
    layer_count, width, _ = weights.shape
    rows = cot.shape[0]
    return pl.pallas_call(
        backward_kernel,
        out_shape=jax.ShapeDtypeStruct((layer_count, width, width), bf16),
        in_specs=[SMEM] + [VMEM] * (3 + 2 * layer_count),
        out_specs=VMEM,
        scratch_shapes=[
            pltpu.VMEM((rows, width), f32),
            pltpu.VMEM((rows, width), bf16),
            pltpu.VMEM((rows, width), bf16),
        ],
        compiler_params=pltpu.CompilerParams(vmem_limit_bytes=vmem_limit),
        cost_estimate=pl.CostEstimate(flops=2_000_000_000, bytes_accessed=9_000_000, transcendentals=0),
    )(cols, cot, tiles_t, weights, *supports, *slopes)


def assemble_kernel(replicas, *rest):
    out, sems = rest[-2:]
    pieces = rest[:-2]
    me = lax.axis_index("rep")
    rows = pieces[0].shape[0]
    copies = []
    for i, piece in enumerate(pieces):
        layer, behind = divmod(i, replicas)
        at = lax.rem(me + replicas - behind, replicas) * rows
        copies.append(
            pltpu.make_async_copy(piece, out.at[layer, pl.ds(pl.multiple_of(at, 128), rows), :], sems.at[i])
        )
    for copy in copies:
        copy.start()
    for copy in copies:
        copy.wait()


def assemble(replicas, pieces):
    layers = len(pieces) // replicas
    rows, width = pieces[0].shape
    return pl.pallas_call(
        functools.partial(assemble_kernel, replicas),
        out_shape=jax.ShapeDtypeStruct((layers, replicas * rows, width), bf16),
        in_specs=[ANY] * len(pieces),
        out_specs=ANY,
        scratch_shapes=[pltpu.SemaphoreType.DMA((len(pieces),))],
        cost_estimate=pl.CostEstimate(flops=0, bytes_accessed=12_600_000, transcendentals=0),
    )(*pieces)


def exchange(value, axis):
    return lax.all_to_all(value, axis, split_axis=0, concat_axis=0, tiled=True)


def body(
    features,
    history,
    tiles,
    tile_cols,
    halo_ids,
    halo_counts,
    halo_dst,
    halo_wt,
    weights,
    cotangent,
):
    row_count, width = features.shape
    layer_count = weights.shape[0]
    parts = lax.axis_size("dom")
    replicas = lax.axis_size("rep")
    slot_count = halo_ids.shape[1]
    capacity = slot_count // parts
    slab = history.shape[1]

    wanted = halo_ids.reshape(layer_count, parts, capacity).transpose(1, 0, 2)
    wanted = exchange(wanted.reshape(parts, layer_count * capacity), "dom")
    wanted = wanted.reshape(parts, layer_count, capacity)
    first = history[0].at[wanted[:, 0].reshape(-1)].get(mode="promise_in_bounds")
    first = exchange(first.reshape(parts, capacity, width), "dom")
    shift = (jnp.arange(layer_count, dtype=jnp.int32) * slab)[None, 1:, None]
    later = history.reshape(layer_count * slab, width).at[(wanted[:, 1:] + shift).reshape(-1)].get(
        mode="promise_in_bounds"
    )
    later = exchange(later.reshape(parts, (layer_count - 1) * capacity, width), "dom")
    later = later.reshape(parts, layer_count - 1, capacity, width).transpose(1, 0, 2, 3)
    later = later.reshape(layer_count - 1, slot_count, width)
    pulled = [first.reshape(slot_count, width)] + [later[i] for i in range(layer_count - 1)]

    rank = jnp.arange(capacity, dtype=jnp.int32)
    live = rank[None, None, :] < halo_counts[:, :, None]
    slot_wt = jnp.where(live.reshape(layer_count, slot_count), halo_wt.astype(f32), 0.0)
    tiles_t = tiles.transpose(0, 2, 1)

    hidden = features
    supports, slopes, pieces = [], [], []
    for depth in range(layer_count):
        support_bf, slope, hidden = forward_layer(
            beta_table[depth],
            tile_cols,
            hidden,
            tiles,
            pulled[depth],
            halo_dst[depth][None, :],
            slot_wt[depth][None, :],
            features,
            weights[depth],
        )
        supports.append(support_bf)
        slopes.append(slope)
        if depth + 1 < layer_count:
            pieces.append(hidden)
            for k in range(1, replicas):
                pieces.append(lax.ppermute(hidden, "rep", [(i, (i + k) % replicas) for i in range(replicas)]))
    grads = backward(tile_cols, cotangent, tiles_t, weights, supports, slopes)
    chunk = layer_count * width // parts
    mine = exchange(grads.reshape(parts, chunk, width), "dom").astype(f32).sum(axis=0)
    mine = exchange(jnp.broadcast_to(mine[None], (replicas, chunk, width)), "rep").sum(axis=0)
    whole = exchange(jnp.broadcast_to(mine.astype(bf16)[None], (parts, chunk, width)), "dom")
    weight_grad = whole.astype(f32).reshape(layer_count, width, width)
    new_history = assemble(replicas, pieces)
    return (hidden, new_history, weight_grad)


def solution(mesh):
    in_specs = (
        P(("dom", "rep"), None),
        P(None, "dom", None),
        P(("dom", "rep"), None, None),
        P(("dom", "rep")),
        P(None, ("dom", "rep")),
        P(None, ("dom", "rep")),
        P(None, ("dom", "rep")),
        P(None, ("dom", "rep")),
        P(),
        P(("dom", "rep"), None),
    )
    out_specs = (P(("dom", "rep"), None), P(None, "dom", None), P())
    return jax.shard_map(body, mesh=mesh, in_specs=in_specs, out_specs=out_specs, check_vma=False)
```

```python
import functools

import jax
import jax.numpy as jnp
from jax import lax
from jax.experimental import pallas as pl
from jax.experimental.pallas import tpu as pltpu
from jax.sharding import PartitionSpec as P

restart_rate = 0.1
beta_table = [
    0.4054651081081644,
    0.22314355131420976,
    0.15415067982725836,
    0.11778303565638346,
    0.09531017980432493,
    0.08004270767353637,
    0.06899287148695142,
    0.06062462181643484,
]
f32 = jnp.float32
bf16 = jnp.bfloat16
gelu_c = 0.7978845608028654
gelu_k = 0.044715
row_step = 256
vmem_limit = 58 * 1024 * 1024
VMEM = pl.BlockSpec(memory_space=pltpu.VMEM)
SMEM = pl.BlockSpec(memory_space=pltpu.SMEM)
ANY = pl.BlockSpec(memory_space=pl.ANY)


def pull_kernel(lo, capacity, wanted, history, rows_o, tables, folded, rows, sems):
    count, slab, width = tables.shape
    parts, slots, _ = rows_o.shape
    lanes = width // 2
    unroll = 4
    copies = [pltpu.make_async_copy(history.at[lo + i], tables.at[i], sems.at[i]) for i in range(count)]
    for copy in copies:
        copy.start()
    for layer in range(count):
        copies[layer].wait()
        folded[pl.ds(0, slab, stride=2), :] = tables[layer, :, :lanes].astype(f32)
        folded[pl.ds(1, slab, stride=2), :] = tables[layer, :, lanes:].astype(f32)

        def step(i, carry):
            for u in range(unroll):
                part = i * unroll + u
                base = pl.multiple_of(part * (2 * slots), 16)
                for c in range(capacity):
                    row = pl.multiple_of(2 * wanted[part, (lo + layer) * capacity + c], 2)
                    rows[pl.ds(base + 2 * (layer * capacity + c), 2), :] = folded[pl.ds(row, 2), :]
            return carry

        lax.fori_loop(0, parts // unroll, step, 0)
    for side in range(2):
        half = rows[pl.ds(side, parts * slots, stride=2), :]
        rows_o[:, :, side * lanes : (side + 1) * lanes] = half.reshape(parts, slots, lanes).astype(bf16)


def pull_rows(wanted, history, lo, count, capacity):
    _, slab, width = history.shape
    parts = wanted.shape[0]
    shape = (parts, count * capacity, width)
    return pl.pallas_call(
        functools.partial(pull_kernel, lo, capacity),
        out_shape=jax.ShapeDtypeStruct(shape, bf16),
        in_specs=[SMEM, ANY],
        out_specs=VMEM,
        scratch_shapes=[
            pltpu.VMEM((count, slab, width), bf16),
            pltpu.VMEM((2 * slab, width // 2), f32),
            pltpu.VMEM((2 * parts * count * capacity, width // 2), f32),
            pltpu.SemaphoreType.DMA((count,)),
        ],
        compiler_params=pltpu.CompilerParams(vmem_limit_bytes=vmem_limit),
        cost_estimate=pl.CostEstimate(flops=0, bytes_accessed=20_000_000, transcendentals=0),
    )(wanted, history)


def window(index, capacity):
    start = index * capacity // 16 * 16
    stop = -(-(index + 1) * capacity // 16) * 16
    return start, stop


def forward_math(depth, lo16, hi16, cols, hidden, tiles, pulled, dst, wt, features, weights, support_o, slope_o, hidden_o):
    beta = beta_table[depth]
    parts, _, width = pulled.shape
    slots = parts * (hi16 - lo16)
    row_count = features.shape[0]
    step = row_step
    per_block = tiles.shape[0] // (row_count // 128)
    dst_row = dst[depth : depth + 1, :]
    wt_row = wt[depth : depth + 1, :]
    for chunk in range(row_count // step):
        lo = chunk * step
        position = lax.broadcasted_iota(jnp.int32, (step, slots), 0) + lo
        scatter = jnp.where(dst_row == position, wt_row, 0.0).astype(bf16)
        acc = jnp.dot(
            scatter, pulled[:, lo16:hi16, :].reshape(slots, width), preferred_element_type=f32
        )
        parts_of = []
        for block in range(lo // 128, (lo + step) // 128):
            picked = jnp.concatenate(
                [
                    hidden[pl.ds(pl.multiple_of(cols[block * per_block + k] * 128, 128), 128), :]
                    for k in range(per_block)
                ],
                axis=0,
            )
            tile_row = jnp.concatenate([tiles[block * per_block + k] for k in range(per_block)], axis=1)
            parts_of.append(jnp.dot(tile_row, picked, preferred_element_type=f32))
        acc = acc + jnp.concatenate(parts_of, axis=0)
        support = (1.0 - restart_rate) * acc + restart_rate * features[lo : lo + step, :].astype(f32)
        support_bf = support.astype(bf16)
        support_o[lo : lo + step, :] = support_bf
        pre = (1.0 - beta) * support + beta * jnp.dot(
            support_bf, weights[depth], preferred_element_type=f32
        )
        square = pre * pre
        th = jnp.tanh(gelu_c * (pre + gelu_k * pre * square))
        half = 0.5 * (1.0 + th)
        hidden_o[lo : lo + step, :] = (pre * half).astype(bf16)
        slope_o[lo : lo + step, :] = half + 0.5 * pre * (1.0 - th * th) * (
            gelu_c * (1.0 + 3.0 * gelu_k * square)
        )


def forward_layer(depth, slots16, cols, hidden, tiles, pulled, dst, wt, features, weights):
    rows, width = features.shape
    return pl.pallas_call(
        functools.partial(forward_math, depth, *slots16),
        out_shape=(
            jax.ShapeDtypeStruct((rows, width), bf16),
            jax.ShapeDtypeStruct((rows, width), f32),
            jax.ShapeDtypeStruct((rows, width), bf16),
        ),
        in_specs=[SMEM] + [VMEM] * 7,
        out_specs=(VMEM, VMEM, VMEM),
        compiler_params=pltpu.CompilerParams(vmem_limit_bytes=vmem_limit),
        cost_estimate=pl.CostEstimate(flops=1_300_000_000, bytes_accessed=6_000_000, transcendentals=262144),
    )(cols, hidden, tiles, pulled, dst, wt, features, weights)


def finish_kernel(half, windows, *refs):
    cols, hidden, pulled, dst, wt, weights = refs[:6]
    count = 4 + 2 * half
    away, refs = refs[6 : 6 + count], refs[6 + count :]
    fresh, grads_o, refs = refs[:half], refs[half], refs[half + 1 :]
    held, refs = refs[:count], refs[count:]
    supports = held[4 : 4 + half] + refs[:half]
    slopes = held[4 + half :] + refs[half : 2 * half]
    total, grad_bf, gs_bf, sems = refs[2 * half :]
    tiles, features, cot, tiles_t = held[:4]
    copies = [pltpu.make_async_copy(a, b, sems.at[i]) for i, (a, b) in enumerate(zip(away, held))]
    for copy in copies:
        copy.start()
    copies[0].wait()
    copies[1].wait()
    for i in range(half):
        depth = half + i
        forward_math(
            depth, *windows[i], cols, hidden, tiles, pulled, dst, wt, features, weights,
            supports[depth], slopes[depth], fresh[i],
        )
        hidden = fresh[i]
    for copy in copies[2:]:
        copy.wait()
    backward_math(cols, cot, tiles_t, weights, supports, slopes, grads_o, total, grad_bf, gs_bf)


def backward_math(cols, cot, tiles_t, weights, supports, slopes, grads_o, total, grad_bf, gs_bf):
    layer_count = weights.shape[0]
    row_count, width = cot.shape
    step = row_step
    per_block = tiles_t.shape[0] // (row_count // 128)
    for depth in range(layer_count - 1, -1, -1):
        beta = beta_table[depth]
        weight = weights[depth]
        for chunk in range(row_count // step):
            lo = chunk * step
            if depth == layer_count - 1:
                grad_out = cot[lo : lo + step, :].astype(f32)
            else:
                grad_out = ((1.0 - restart_rate) * total[lo : lo + step, :]).astype(bf16).astype(f32)
            gp = grad_out * slopes[depth][lo : lo + step, :]
            gp_bf = gp.astype(bf16)
            grad_bf[lo : lo + step, :] = gp_bf
            if depth > 0:
                gs = (1.0 - beta) * gp + beta * lax.dot_general(
                    gp_bf, weight, (((1,), (1,)), ((), ())), preferred_element_type=f32
                )
                gs_bf[lo : lo + step, :] = gs.astype(bf16)
        grads_o[depth] = (
            beta
            * lax.dot_general(
                supports[depth][...], grad_bf[...], (((0,), (0,)), ((), ())), preferred_element_type=f32
            )
        ).astype(bf16)
        if depth > 0:
            total[...] = jnp.zeros_like(total)
            for block in range(row_count // 128):
                tile_col = jnp.concatenate(
                    [tiles_t[block * per_block + k] for k in range(per_block)], axis=0
                )
                product = jnp.dot(
                    tile_col, gs_bf[block * 128 : (block + 1) * 128, :], preferred_element_type=f32
                )
                for k in range(per_block):
                    at = pl.ds(pl.multiple_of(cols[block * per_block + k] * 128, 128), 128)
                    total[at, :] = total[at, :] + product[k * 128 : (k + 1) * 128, :]


def finish(half, windows, cols, hidden, pulled, dst, wt, weights, tiles, features, cot, tiles_t, supports, slopes):
    layer_count, width, _ = weights.shape
    away = [tiles, features, cot, tiles_t, *supports, *slopes]
    block = jax.ShapeDtypeStruct(features.shape, bf16)
    new = layer_count - half
    outs = pl.pallas_call(
        functools.partial(finish_kernel, half, windows),
        out_shape=(block,) * new + (jax.ShapeDtypeStruct((layer_count, width, width), bf16),),
        in_specs=[SMEM] + [VMEM] * 5 + [ANY] * len(away),
        out_specs=(VMEM,) * (new + 1),
        scratch_shapes=[pltpu.VMEM(a.shape, a.dtype) for a in away]
        + [pltpu.VMEM(features.shape, bf16)] * new
        + [pltpu.VMEM(features.shape, f32)] * new
        + [
            pltpu.VMEM(features.shape, f32),
            pltpu.VMEM(features.shape, bf16),
            pltpu.VMEM(features.shape, bf16),
            pltpu.SemaphoreType.DMA((len(away),)),
        ],
        compiler_params=pltpu.CompilerParams(vmem_limit_bytes=vmem_limit),
        cost_estimate=pl.CostEstimate(flops=5_000_000_000, bytes_accessed=12_000_000, transcendentals=524288),
    )(cols, hidden, pulled, dst, wt, weights, *away)
    return outs[:new], outs[new]


def assemble_kernel(places, replicas, rows, count, *refs):
    pieces = refs[:count]
    out, sems = refs[-2:]
    me = lax.axis_index("rep")
    copies = []
    for i, (layer, ahead, offset) in enumerate(places):
        at = lax.rem(me + ahead, replicas) * rows + offset
        size = pieces[i].shape[0]
        copies.append(
            pltpu.make_async_copy(
                pieces[i], out.at[layer, pl.ds(pl.multiple_of(at, 128), size), :], sems.at[i]
            )
        )
    for copy in copies:
        copy.start()
    for copy in copies:
        copy.wait()


def assemble(layers, replicas, rows, pieces, so_far):
    places = [piece[:3] for piece in pieces]
    blocks = [piece[3] for piece in pieces]
    width = blocks[0].shape[1]
    extra = [] if so_far is None else [so_far]
    return pl.pallas_call(
        functools.partial(assemble_kernel, places, replicas, rows, len(blocks)),
        out_shape=jax.ShapeDtypeStruct((layers, replicas * rows, width), bf16),
        in_specs=[VMEM] * len(blocks) + [ANY] * len(extra),
        out_specs=ANY,
        input_output_aliases={len(blocks): 0} if extra else {},
        scratch_shapes=[pltpu.SemaphoreType.DMA((len(blocks),))],
        cost_estimate=pl.CostEstimate(flops=0, bytes_accessed=4_200_000, transcendentals=0),
    )(*blocks, *extra)


def move(value, by):
    size = lax.axis_size("rep")
    return lax.ppermute(value, "rep", [(i, (i + by) % size) for i in range(size)])


def send_near(value):
    return [move(value, 1), move(value, -1)]


def send_far(near):
    half = near[0].shape[0] // 2
    return [move(near[0][:half], 1), move(near[1][half:], -1)]


def exchange(value, axis):
    return lax.all_to_all(value, axis, split_axis=0, concat_axis=0, tiled=True)


def body(
    features,
    history,
    tiles,
    tile_cols,
    halo_ids,
    halo_counts,
    halo_dst,
    halo_wt,
    weights,
    cotangent,
):
    row_count, width = features.shape
    layer_count = weights.shape[0]
    parts = lax.axis_size("dom")
    replicas = lax.axis_size("rep")
    slot_count = halo_ids.shape[1]
    capacity = slot_count // parts
    slab = history.shape[1]

    half = layer_count // 2

    wanted = halo_ids.reshape(layer_count, parts, capacity).transpose(1, 0, 2)
    wanted = exchange(wanted.reshape(parts, layer_count * capacity), "dom")
    early = exchange(pull_rows(wanted, history, 0, half, capacity), "dom")
    later = exchange(pull_rows(wanted, history, half, half, capacity), "dom")

    rank = jnp.arange(capacity, dtype=jnp.int32)
    live = rank[None, None, :] < halo_counts[:, :, None]
    slot_wt = jnp.where(live, halo_wt.reshape(layer_count, parts, capacity).astype(f32), 0.0)
    slot_dst = halo_dst.reshape(layer_count, parts, capacity)
    windows = [window(i, capacity) for i in range(half)]
    spread_dst, spread_wt = [], []
    for depth in range(layer_count):
        start, stop = windows[depth % half]
        before = depth % half * capacity - start
        pad = ((0, 0), (before, stop - start - capacity - before))
        spread_dst.append(jnp.pad(slot_dst[depth], pad).reshape(-1))
        spread_wt.append(jnp.pad(slot_wt[depth], pad).reshape(-1))
    dst = jnp.stack(spread_dst)
    wt = jnp.stack(spread_wt)
    tiles_t = tiles.transpose(0, 2, 1)

    hidden = features
    supports, slopes, fresh = [], [], []
    for depth in range(half):
        support_bf, slope, hidden = forward_layer(
            depth, windows[depth], tile_cols, hidden, tiles, early, dst, wt, features, weights
        )
        supports.append(support_bf)
        slopes.append(slope)
        fresh.append(hidden)
    near = [send_near(fresh[0]), send_near(hidden)]
    near[0], hidden = lax.optimization_barrier((near[0], hidden))
    far = [send_far(near[0])]
    later, near[1], far[0] = lax.optimization_barrier((later, near[1], far[0]))
    last, grads = finish(
        half, windows, tile_cols, hidden, later, dst, wt, weights,
        tiles, features, cotangent, tiles_t, supports, slopes,
    )
    fresh.append(last[0])
    hidden = last[1]
    near.append(send_near(fresh[2]))
    far.append(send_far(near[1]))
    chunk = layer_count * width // parts
    mine = exchange(grads.reshape(parts, chunk, width), "dom")
    mine, far[1], near[2] = lax.optimization_barrier((mine, far[1], near[2]))
    far.append(send_far(near[2]))
    mine = mine.astype(f32).sum(axis=0)
    mine = exchange(jnp.broadcast_to(mine[None], (replicas, chunk, width)), "rep")
    mine = mine.sum(axis=0)
    whole = exchange(jnp.broadcast_to(mine.astype(bf16)[None], (parts, chunk, width)), "dom")
    weight_grad = whole.astype(f32).reshape(layer_count, width, width)
    first, second = [], []
    for layer in range(layer_count - 1):
        first += [(layer, 0, 0, fresh[layer]), (layer, replicas - 1, 0, near[layer][0]), (layer, 1, 0, near[layer][1])]
        (second if layer + 2 == layer_count else first).extend(
            [(layer, 2, 0, far[layer][0]), (layer, 2, row_count // 2, far[layer][1])]
        )
    new_history = assemble(layer_count - 1, replicas, row_count, first, None)
    new_history = assemble(layer_count - 1, replicas, row_count, second, new_history)
    return (hidden, new_history, weight_grad)


def solution(mesh):
    in_specs = (
        P(("dom", "rep"), None),
        P(None, "dom", None),
        P(("dom", "rep"), None, None),
        P(("dom", "rep")),
        P(None, ("dom", "rep")),
        P(None, ("dom", "rep")),
        P(None, ("dom", "rep")),
        P(None, ("dom", "rep")),
        P(),
        P(("dom", "rep"), None),
    )
    out_specs = (P(("dom", "rep"), None), P(None, "dom", None), P())
    return jax.shard_map(body, mesh=mesh, in_specs=in_specs, out_specs=out_specs, check_vma=False)
```

```python
import functools

import jax
import jax.numpy as jnp
from jax import lax
from jax.experimental import pallas as pl
from jax.experimental.pallas import tpu as pltpu
from jax.sharding import PartitionSpec as P

restart_rate = 0.1
beta_table = [
    0.4054651081081644,
    0.22314355131420976,
    0.15415067982725836,
    0.11778303565638346,
    0.09531017980432493,
    0.08004270767353637,
    0.06899287148695142,
    0.06062462181643484,
]
f32 = jnp.float32
bf16 = jnp.bfloat16
gelu_c = 0.7978845608028654
gelu_k = 0.044715
row_step = 512
vmem_limit = 58 * 1024 * 1024
VMEM = pl.BlockSpec(memory_space=pltpu.VMEM)
SMEM = pl.BlockSpec(memory_space=pltpu.SMEM)
ANY = pl.BlockSpec(memory_space=pl.ANY)


def pull_kernel(lo, capacity, wanted, history, rows_o, tables, folded, rows, sems):
    count, slab, width = tables.shape
    parts, slots, _ = rows_o.shape
    lanes = width // 2
    unroll = 4
    copies = [pltpu.make_async_copy(history.at[lo + i], tables.at[i], sems.at[i]) for i in range(count)]
    for copy in copies:
        copy.start()
    for layer in range(count):
        copies[layer].wait()
        folded[pl.ds(0, slab, stride=2), :] = tables[layer, :, :lanes].astype(f32)
        folded[pl.ds(1, slab, stride=2), :] = tables[layer, :, lanes:].astype(f32)

        def step(i, carry):
            for u in range(unroll):
                part = i * unroll + u
                base = pl.multiple_of(part * (2 * slots), 16)
                for c in range(capacity):
                    row = pl.multiple_of(2 * wanted[part, (lo + layer) * capacity + c], 2)
                    rows[pl.ds(base + 2 * (layer * capacity + c), 2), :] = folded[pl.ds(row, 2), :]
            return carry

        lax.fori_loop(0, parts // unroll, step, 0)
    for side in range(2):
        half = rows[pl.ds(side, parts * slots, stride=2), :]
        rows_o[:, :, side * lanes : (side + 1) * lanes] = half.reshape(parts, slots, lanes).astype(bf16)


def pull_rows(wanted, history, lo, count, capacity):
    _, slab, width = history.shape
    parts = wanted.shape[0]
    shape = (parts, count * capacity, width)
    return pl.pallas_call(
        functools.partial(pull_kernel, lo, capacity),
        out_shape=jax.ShapeDtypeStruct(shape, bf16),
        in_specs=[SMEM, ANY],
        out_specs=VMEM,
        scratch_shapes=[
            pltpu.VMEM((count, slab, width), bf16),
            pltpu.VMEM((2 * slab, width // 2), f32),
            pltpu.VMEM((2 * parts * count * capacity, width // 2), f32),
            pltpu.SemaphoreType.DMA((count,)),
        ],
        compiler_params=pltpu.CompilerParams(vmem_limit_bytes=vmem_limit),
        cost_estimate=pl.CostEstimate(flops=0, bytes_accessed=20_000_000, transcendentals=0),
    )(wanted, history)


def forward_math(depth, at, cols, hidden, tiles, pulled, dst, wt, features, weights, support_o, slope_o, hidden_o):
    beta = beta_table[depth]
    parts, _, width = pulled.shape
    slots = dst.shape[1]
    capacity = slots // parts
    row_count = features.shape[0]
    step = row_step
    per_block = tiles.shape[0] // (row_count // 128)
    dst_row = dst[depth : depth + 1, :]
    wt_row = wt[depth : depth + 1, :]
    for chunk in range(row_count // step):
        lo = chunk * step
        position = lax.broadcasted_iota(jnp.int32, (step, slots), 0) + lo
        scatter = jnp.where(dst_row == position, wt_row, 0.0).astype(bf16)
        acc = jnp.dot(
            scatter,
            pulled[:, at * capacity : (at + 1) * capacity, :].reshape(slots, width),
            preferred_element_type=f32,
        )
        parts_of = []
        for block in range(lo // 128, (lo + step) // 128):
            picked = jnp.concatenate(
                [
                    hidden[pl.ds(pl.multiple_of(cols[block * per_block + k] * 128, 128), 128), :]
                    for k in range(per_block)
                ],
                axis=0,
            )
            tile_row = jnp.concatenate([tiles[block * per_block + k] for k in range(per_block)], axis=1)
            parts_of.append(jnp.dot(tile_row, picked, preferred_element_type=f32))
        acc = acc + jnp.concatenate(parts_of, axis=0)
        support = (1.0 - restart_rate) * acc + restart_rate * features[lo : lo + step, :].astype(f32)
        support_bf = support.astype(bf16)
        support_o[lo : lo + step, :] = support_bf
        pre = (1.0 - beta) * support + beta * jnp.dot(
            support_bf, weights[depth], preferred_element_type=f32
        )
        square = pre * pre
        th = jnp.tanh(gelu_c * (pre + gelu_k * pre * square))
        half = 0.5 * (1.0 + th)
        hidden_o[lo : lo + step, :] = (pre * half).astype(bf16)
        slope_o[lo : lo + step, :] = half + 0.5 * pre * (1.0 - th * th) * (
            gelu_c * (1.0 + 3.0 * gelu_k * square)
        )


def forward_layer(depth, at, cols, hidden, tiles, pulled, dst, wt, features, weights):
    rows, width = features.shape
    return pl.pallas_call(
        functools.partial(forward_math, depth, at),
        out_shape=(
            jax.ShapeDtypeStruct((rows, width), bf16),
            jax.ShapeDtypeStruct((rows, width), f32),
            jax.ShapeDtypeStruct((rows, width), bf16),
        ),
        in_specs=[SMEM] + [VMEM] * 7,
        out_specs=(VMEM, VMEM, VMEM),
        compiler_params=pltpu.CompilerParams(vmem_limit_bytes=vmem_limit),
        cost_estimate=pl.CostEstimate(flops=1_300_000_000, bytes_accessed=6_000_000, transcendentals=262144),
    )(cols, hidden, tiles, pulled, dst, wt, features, weights)


def finish_kernel(half, *refs):
    cols, hidden, pulled, dst, wt, weights = refs[:6]
    count = 4 + 2 * half
    away, refs = refs[6 : 6 + count], refs[6 + count :]
    fresh, grads_o, refs = refs[:half], refs[half], refs[half + 1 :]
    held, refs = refs[:count], refs[count:]
    supports = held[4 : 4 + half] + refs[:half]
    slopes = held[4 + half :] + refs[half : 2 * half]
    total, grad_bf, gs_bf, sems = refs[2 * half :]
    tiles, features, cot, tiles_t = held[:4]
    copies = [pltpu.make_async_copy(a, b, sems.at[i]) for i, (a, b) in enumerate(zip(away, held))]
    for copy in copies:
        copy.start()
    copies[0].wait()
    copies[1].wait()
    for i in range(half):
        depth = half + i
        forward_math(
            depth, i, cols, hidden, tiles, pulled, dst, wt, features, weights,
            supports[depth], slopes[depth], fresh[i],
        )
        hidden = fresh[i]
    for copy in copies[2:]:
        copy.wait()
    backward_math(cols, cot, tiles_t, weights, supports, slopes, grads_o, total, grad_bf, gs_bf)


def backward_math(cols, cot, tiles_t, weights, supports, slopes, grads_o, total, grad_bf, gs_bf):
    layer_count = weights.shape[0]
    row_count, width = cot.shape
    step = row_step
    per_block = tiles_t.shape[0] // (row_count // 128)
    for depth in range(layer_count - 1, -1, -1):
        beta = beta_table[depth]
        weight = weights[depth]
        for chunk in range(row_count // step):
            lo = chunk * step
            if depth == layer_count - 1:
                grad_out = cot[lo : lo + step, :].astype(f32)
            else:
                grad_out = ((1.0 - restart_rate) * total[lo : lo + step, :]).astype(bf16).astype(f32)
            gp = grad_out * slopes[depth][lo : lo + step, :]
            gp_bf = gp.astype(bf16)
            grad_bf[lo : lo + step, :] = gp_bf
            if depth > 0:
                gs = (1.0 - beta) * gp + beta * lax.dot_general(
                    gp_bf, weight, (((1,), (1,)), ((), ())), preferred_element_type=f32
                )
                gs_bf[lo : lo + step, :] = gs.astype(bf16)
        grads_o[depth] = (
            beta
            * lax.dot_general(
                supports[depth][...], grad_bf[...], (((0,), (0,)), ((), ())), preferred_element_type=f32
            )
        ).astype(bf16)
        if depth > 0:
            total[...] = jnp.zeros_like(total)
            for block in range(row_count // 128):
                tile_col = jnp.concatenate(
                    [tiles_t[block * per_block + k] for k in range(per_block)], axis=0
                )
                product = jnp.dot(
                    tile_col, gs_bf[block * 128 : (block + 1) * 128, :], preferred_element_type=f32
                )
                for k in range(per_block):
                    at = pl.ds(pl.multiple_of(cols[block * per_block + k] * 128, 128), 128)
                    total[at, :] = total[at, :] + product[k * 128 : (k + 1) * 128, :]


def finish(half, cols, hidden, pulled, dst, wt, weights, tiles, features, cot, tiles_t, supports, slopes):
    layer_count, width, _ = weights.shape
    away = [tiles, features, cot, tiles_t, *supports, *slopes]
    block = jax.ShapeDtypeStruct(features.shape, bf16)
    new = layer_count - half
    outs = pl.pallas_call(
        functools.partial(finish_kernel, half),
        out_shape=(block,) * new + (jax.ShapeDtypeStruct((layer_count, width, width), bf16),),
        in_specs=[SMEM] + [VMEM] * 5 + [ANY] * len(away),
        out_specs=(VMEM,) * (new + 1),
        scratch_shapes=[pltpu.VMEM(a.shape, a.dtype) for a in away]
        + [pltpu.VMEM(features.shape, bf16)] * new
        + [pltpu.VMEM(features.shape, f32)] * new
        + [
            pltpu.VMEM(features.shape, f32),
            pltpu.VMEM(features.shape, bf16),
            pltpu.VMEM(features.shape, bf16),
            pltpu.SemaphoreType.DMA((len(away),)),
        ],
        compiler_params=pltpu.CompilerParams(vmem_limit_bytes=vmem_limit),
        cost_estimate=pl.CostEstimate(flops=5_000_000_000, bytes_accessed=12_000_000, transcendentals=524288),
    )(cols, hidden, pulled, dst, wt, weights, *away)
    return outs[:new], outs[new]


def assemble_kernel(places, replicas, rows, count, *refs):
    pieces = refs[:count]
    out, sems = refs[-2:]
    me = lax.axis_index("rep")
    copies = []
    for i, (layer, ahead, offset) in enumerate(places):
        at = lax.rem(me + ahead, replicas) * rows + offset
        size = pieces[i].shape[0]
        copies.append(
            pltpu.make_async_copy(
                pieces[i], out.at[layer, pl.ds(pl.multiple_of(at, 128), size), :], sems.at[i]
            )
        )
    for copy in copies:
        copy.start()
    for copy in copies:
        copy.wait()


def assemble(layers, replicas, rows, pieces, so_far):
    places = [piece[:3] for piece in pieces]
    blocks = [piece[3] for piece in pieces]
    width = blocks[0].shape[1]
    extra = [] if so_far is None else [so_far]
    return pl.pallas_call(
        functools.partial(assemble_kernel, places, replicas, rows, len(blocks)),
        out_shape=jax.ShapeDtypeStruct((layers, replicas * rows, width), bf16),
        in_specs=[VMEM] * len(blocks) + [ANY] * len(extra),
        out_specs=ANY,
        input_output_aliases={len(blocks): 0} if extra else {},
        scratch_shapes=[pltpu.SemaphoreType.DMA((len(blocks),))],
        cost_estimate=pl.CostEstimate(flops=0, bytes_accessed=4_200_000, transcendentals=0),
    )(*blocks, *extra)


def move(value, by):
    size = lax.axis_size("rep")
    return lax.ppermute(value, "rep", [(i, (i + by) % size) for i in range(size)])


def send_near(value):
    return [move(value, 1), move(value, -1)]


def send_far(near):
    half = near[0].shape[0] // 2
    return [move(near[0][:half], 1), move(near[1][half:], -1)]


def exchange(value, axis):
    return lax.all_to_all(value, axis, split_axis=0, concat_axis=0, tiled=True)


def body(
    features,
    history,
    tiles,
    tile_cols,
    halo_ids,
    halo_counts,
    halo_dst,
    halo_wt,
    weights,
    cotangent,
):
    row_count, width = features.shape
    layer_count = weights.shape[0]
    parts = lax.axis_size("dom")
    replicas = lax.axis_size("rep")
    slot_count = halo_ids.shape[1]
    capacity = slot_count // parts
    slab = history.shape[1]

    half = layer_count // 2

    wanted = halo_ids.reshape(layer_count, parts, capacity).transpose(1, 0, 2)
    wanted = exchange(wanted.reshape(parts, layer_count * capacity), "dom")
    early = exchange(pull_rows(wanted, history, 0, half, capacity), "dom")
    later = exchange(pull_rows(wanted, history, half, half, capacity), "dom")

    rank = jnp.arange(capacity, dtype=jnp.int32)
    live = rank[None, None, :] < halo_counts[:, :, None]
    wt = jnp.where(live.reshape(layer_count, slot_count), halo_wt.astype(f32), 0.0)
    tiles_t = tiles.transpose(0, 2, 1)

    hidden = features
    supports, slopes, fresh = [], [], []
    for depth in range(half):
        support_bf, slope, hidden = forward_layer(
            depth, depth, tile_cols, hidden, tiles, early, halo_dst, wt, features, weights
        )
        supports.append(support_bf)
        slopes.append(slope)
        fresh.append(hidden)
    near = [send_near(fresh[0]), send_near(hidden)]
    near[0], hidden = lax.optimization_barrier((near[0], hidden))
    far = [send_far(near[0])]
    later, near[1], far[0] = lax.optimization_barrier((later, near[1], far[0]))
    last, grads = finish(
        half, tile_cols, hidden, later, halo_dst, wt, weights,
        tiles, features, cotangent, tiles_t, supports, slopes,
    )
    fresh.append(last[0])
    hidden = last[1]
    near.append(send_near(fresh[2]))
    far.append(send_far(near[1]))
    chunk = layer_count * width // parts
    mine = exchange(grads.reshape(parts, chunk, width), "dom")
    mine, near[2] = lax.optimization_barrier((mine, near[2]))
    far.append(send_far(near[2]))
    mine = mine.astype(f32).sum(axis=0)
    mine = exchange(jnp.broadcast_to(mine[None], (replicas, chunk, width)), "rep")
    mine = mine.sum(axis=0)
    whole = exchange(jnp.broadcast_to(mine.astype(bf16)[None], (parts, chunk, width)), "dom")
    weight_grad = whole.astype(f32).reshape(layer_count, width, width)
    first, second = [], []
    for layer in range(layer_count - 1):
        first += [(layer, 0, 0, fresh[layer]), (layer, replicas - 1, 0, near[layer][0]), (layer, 1, 0, near[layer][1])]
        (second if layer > 0 else first).extend(
            [(layer, 2, 0, far[layer][0]), (layer, 2, row_count // 2, far[layer][1])]
        )
    new_history = assemble(layer_count - 1, replicas, row_count, first, None)
    new_history = assemble(layer_count - 1, replicas, row_count, second, new_history)
    return (hidden, new_history, weight_grad)


def solution(mesh):
    in_specs = (
        P(("dom", "rep"), None),
        P(None, "dom", None),
        P(("dom", "rep"), None, None),
        P(("dom", "rep")),
        P(None, ("dom", "rep")),
        P(None, ("dom", "rep")),
        P(None, ("dom", "rep")),
        P(None, ("dom", "rep")),
        P(),
        P(("dom", "rep"), None),
    )
    out_specs = (P(("dom", "rep"), None), P(None, "dom", None), P())
    return jax.shard_map(body, mesh=mesh, in_specs=in_specs, out_specs=out_specs, check_vma=False)
```

```python
import functools

import jax
import jax.numpy as jnp
from jax import lax
from jax.experimental import pallas as pl
from jax.experimental.pallas import tpu as pltpu
from jax.sharding import PartitionSpec as P

restart_rate = 0.1
beta_table = [
    0.4054651081081644,
    0.22314355131420976,
    0.15415067982725836,
    0.11778303565638346,
    0.09531017980432493,
    0.08004270767353637,
    0.06899287148695142,
    0.06062462181643484,
]
f32 = jnp.float32
bf16 = jnp.bfloat16
gelu_c = 0.7978845608028654
gelu_k = 0.044715
row_step = 512
vmem_limit = 58 * 1024 * 1024
layer_vmem_limit = 46 * 1024 * 1024
VMEM = pl.BlockSpec(memory_space=pltpu.VMEM)
SMEM = pl.BlockSpec(memory_space=pltpu.SMEM)
ANY = pl.BlockSpec(memory_space=pl.ANY)


def pull_kernel(lo, capacity, wanted, history, rows_o, tables, folded, rows, sems):
    count, slab, width = tables.shape
    parts, slots, _ = rows_o.shape
    lanes = width // 2
    unroll = 4
    copies = [pltpu.make_async_copy(history.at[lo + i], tables.at[i], sems.at[i]) for i in range(count)]
    for copy in copies:
        copy.start()
    for layer in range(count):
        copies[layer].wait()
        folded[pl.ds(0, slab, stride=2), :] = tables[layer, :, :lanes].astype(f32)
        folded[pl.ds(1, slab, stride=2), :] = tables[layer, :, lanes:].astype(f32)

        def step(i, carry):
            for u in range(unroll):
                part = i * unroll + u
                base = pl.multiple_of(part * (2 * slots), 16)
                for c in range(capacity):
                    row = pl.multiple_of(2 * wanted[part, (lo + layer) * capacity + c], 2)
                    rows[pl.ds(base + 2 * (layer * capacity + c), 2), :] = folded[pl.ds(row, 2), :]
            return carry

        lax.fori_loop(0, parts // unroll, step, 0)
    for side in range(2):
        half = rows[pl.ds(side, parts * slots, stride=2), :]
        rows_o[:, :, side * lanes : (side + 1) * lanes] = half.reshape(parts, slots, lanes).astype(bf16)


def pull_rows(wanted, history, lo, count, capacity):
    _, slab, width = history.shape
    parts = wanted.shape[0]
    shape = (parts, count * capacity, width)
    return pl.pallas_call(
        functools.partial(pull_kernel, lo, capacity),
        out_shape=jax.ShapeDtypeStruct(shape, bf16),
        in_specs=[SMEM, ANY],
        out_specs=VMEM,
        scratch_shapes=[
            pltpu.VMEM((count, slab, width), bf16),
            pltpu.VMEM((2 * slab, width // 2), f32),
            pltpu.VMEM((2 * parts * count * capacity, width // 2), f32),
            pltpu.SemaphoreType.DMA((count,)),
        ],
        compiler_params=pltpu.CompilerParams(vmem_limit_bytes=vmem_limit),
        cost_estimate=pl.CostEstimate(flops=0, bytes_accessed=20_000_000, transcendentals=0),
    )(wanted, history)


def forward_math(depth, at, cols, hidden, tiles, pulled, dst, wt, features, weights, support_o, slope_o, hidden_o):
    beta = beta_table[depth]
    parts, _, width = pulled.shape
    slots = dst.shape[1]
    capacity = slots // parts
    row_count = features.shape[0]
    step = row_step
    per_block = tiles.shape[0] // (row_count // 128)
    dst_row = dst[depth : depth + 1, :]
    wt_row = wt[depth : depth + 1, :]
    for chunk in range(row_count // step):
        lo = chunk * step
        position = lax.broadcasted_iota(jnp.int32, (step, slots), 0) + lo
        scatter = jnp.where(dst_row == position, wt_row, 0.0).astype(bf16)
        acc = jnp.dot(
            scatter,
            pulled[:, at * capacity : (at + 1) * capacity, :].reshape(slots, width),
            preferred_element_type=f32,
        )
        parts_of = []
        for block in range(lo // 128, (lo + step) // 128):
            picked = jnp.concatenate(
                [
                    hidden[pl.ds(pl.multiple_of(cols[block * per_block + k] * 128, 128), 128), :]
                    for k in range(per_block)
                ],
                axis=0,
            )
            tile_row = jnp.concatenate([tiles[block * per_block + k] for k in range(per_block)], axis=1)
            parts_of.append(jnp.dot(tile_row, picked, preferred_element_type=f32))
        acc = acc + jnp.concatenate(parts_of, axis=0)
        support = (1.0 - restart_rate) * acc + restart_rate * features[lo : lo + step, :].astype(f32)
        support_bf = support.astype(bf16)
        support_o[lo : lo + step, :] = support_bf
        pre = (1.0 - beta) * support + beta * jnp.dot(
            support_bf, weights[depth], preferred_element_type=f32
        )
        square = pre * pre
        th = jnp.tanh(gelu_c * (pre + gelu_k * pre * square))
        half = 0.5 * (1.0 + th)
        hidden_o[lo : lo + step, :] = (pre * half).astype(bf16)
        slope_o[lo : lo + step, :] = half + 0.5 * pre * (1.0 - th * th) * (
            gelu_c * (1.0 + 3.0 * gelu_k * square)
        )


def forward_layer(depth, at, cols, hidden, tiles, pulled, dst, wt, features, weights):
    rows, width = features.shape
    return pl.pallas_call(
        functools.partial(forward_math, depth, at),
        out_shape=(
            jax.ShapeDtypeStruct((rows, width), bf16),
            jax.ShapeDtypeStruct((rows, width), f32),
            jax.ShapeDtypeStruct((rows, width), bf16),
        ),
        in_specs=[SMEM] + [VMEM] * 7,
        out_specs=(VMEM, VMEM, VMEM),
        compiler_params=pltpu.CompilerParams(vmem_limit_bytes=layer_vmem_limit),
        cost_estimate=pl.CostEstimate(flops=1_300_000_000, bytes_accessed=6_000_000, transcendentals=262144),
    )(cols, hidden, tiles, pulled, dst, wt, features, weights)


def finish_kernel(half, *refs):
    cols, hidden, pulled, dst, wt, weights = refs[:6]
    count = 4 + 2 * half
    away, refs = refs[6 : 6 + count], refs[6 + count :]
    fresh, grads_o, refs = refs[:half], refs[half], refs[half + 1 :]
    held, refs = refs[:count], refs[count:]
    supports = held[4 : 4 + half] + refs[:half]
    slopes = held[4 + half :] + refs[half : 2 * half]
    total, grad_bf, gs_bf, sems = refs[2 * half :]
    tiles, features, cot, tiles_t = held[:4]
    copies = [pltpu.make_async_copy(a, b, sems.at[i]) for i, (a, b) in enumerate(zip(away, held))]
    for copy in copies:
        copy.start()
    copies[0].wait()
    copies[1].wait()
    for i in range(half):
        depth = half + i
        forward_math(
            depth, i, cols, hidden, tiles, pulled, dst, wt, features, weights,
            supports[depth], slopes[depth], fresh[i],
        )
        hidden = fresh[i]
    for copy in copies[2:]:
        copy.wait()
    backward_math(cols, cot, tiles_t, weights, supports, slopes, grads_o, total, grad_bf, gs_bf)


def backward_math(cols, cot, tiles_t, weights, supports, slopes, grads_o, total, grad_bf, gs_bf):
    layer_count = weights.shape[0]
    row_count, width = cot.shape
    step = row_step
    per_block = tiles_t.shape[0] // (row_count // 128)
    for depth in range(layer_count - 1, -1, -1):
        beta = beta_table[depth]
        weight = weights[depth]
        for chunk in range(row_count // step):
            lo = chunk * step
            if depth == layer_count - 1:
                grad_out = cot[lo : lo + step, :].astype(f32)
            else:
                grad_out = ((1.0 - restart_rate) * total[lo : lo + step, :]).astype(bf16).astype(f32)
            gp = grad_out * slopes[depth][lo : lo + step, :]
            gp_bf = gp.astype(bf16)
            grad_bf[lo : lo + step, :] = gp_bf
            if depth > 0:
                gs = (1.0 - beta) * gp + beta * lax.dot_general(
                    gp_bf, weight, (((1,), (1,)), ((), ())), preferred_element_type=f32
                )
                gs_bf[lo : lo + step, :] = gs.astype(bf16)
        grads_o[depth] = (
            beta
            * lax.dot_general(
                supports[depth][...], grad_bf[...], (((0,), (0,)), ((), ())), preferred_element_type=f32
            )
        ).astype(bf16)
        if depth > 0:
            total[...] = jnp.zeros_like(total)
            for block in range(row_count // 128):
                tile_col = jnp.concatenate(
                    [tiles_t[block * per_block + k] for k in range(per_block)], axis=0
                )
                product = jnp.dot(
                    tile_col, gs_bf[block * 128 : (block + 1) * 128, :], preferred_element_type=f32
                )
                for k in range(per_block):
                    at = pl.ds(pl.multiple_of(cols[block * per_block + k] * 128, 128), 128)
                    total[at, :] = total[at, :] + product[k * 128 : (k + 1) * 128, :]


def finish(half, cols, hidden, pulled, dst, wt, weights, tiles, features, cot, tiles_t, supports, slopes):
    layer_count, width, _ = weights.shape
    away = [tiles, features, cot, tiles_t, *supports, *slopes]
    block = jax.ShapeDtypeStruct(features.shape, bf16)
    new = layer_count - half
    outs = pl.pallas_call(
        functools.partial(finish_kernel, half),
        out_shape=(block,) * new + (jax.ShapeDtypeStruct((layer_count, width, width), bf16),),
        in_specs=[SMEM] + [VMEM] * 5 + [ANY] * len(away),
        out_specs=(VMEM,) * (new + 1),
        scratch_shapes=[pltpu.VMEM(a.shape, a.dtype) for a in away]
        + [pltpu.VMEM(features.shape, bf16)] * new
        + [pltpu.VMEM(features.shape, f32)] * new
        + [
            pltpu.VMEM(features.shape, f32),
            pltpu.VMEM(features.shape, bf16),
            pltpu.VMEM(features.shape, bf16),
            pltpu.SemaphoreType.DMA((len(away),)),
        ],
        compiler_params=pltpu.CompilerParams(vmem_limit_bytes=vmem_limit),
        cost_estimate=pl.CostEstimate(flops=5_000_000_000, bytes_accessed=12_000_000, transcendentals=524288),
    )(cols, hidden, pulled, dst, wt, weights, *away)
    return outs[:new], outs[new]


def assemble_kernel(places, replicas, rows, count, *refs):
    pieces = refs[:count]
    out, sems = refs[-2:]
    me = lax.axis_index("rep")
    copies = []
    for i, (layer, ahead, offset) in enumerate(places):
        at = lax.rem(me + ahead, replicas) * rows + offset
        size = pieces[i].shape[0]
        copies.append(
            pltpu.make_async_copy(
                pieces[i], out.at[layer, pl.ds(pl.multiple_of(at, 128), size), :], sems.at[i]
            )
        )
    for copy in copies:
        copy.start()
    for copy in copies:
        copy.wait()


def assemble(layers, replicas, rows, pieces, so_far):
    places = [piece[:3] for piece in pieces]
    blocks = [piece[3] for piece in pieces]
    width = blocks[0].shape[1]
    extra = [] if so_far is None else [so_far]
    return pl.pallas_call(
        functools.partial(assemble_kernel, places, replicas, rows, len(blocks)),
        out_shape=jax.ShapeDtypeStruct((layers, replicas * rows, width), bf16),
        in_specs=[VMEM] * len(blocks) + [ANY] * len(extra),
        out_specs=ANY,
        input_output_aliases={len(blocks): 0} if extra else {},
        scratch_shapes=[pltpu.SemaphoreType.DMA((len(blocks),))],
        cost_estimate=pl.CostEstimate(flops=0, bytes_accessed=4_200_000, transcendentals=0),
    )(*blocks, *extra)


def move(value, by):
    size = lax.axis_size("rep")
    return lax.ppermute(value, "rep", [(i, (i + by) % size) for i in range(size)])


def send_near(value):
    return [move(value, 1), move(value, -1)]


def send_far(near):
    half = near[0].shape[0] // 2
    return [move(near[0][:half], 1), move(near[1][half:], -1)]


def exchange(value, axis):
    return lax.all_to_all(value, axis, split_axis=0, concat_axis=0, tiled=True)


def body(
    features,
    history,
    tiles,
    tile_cols,
    halo_ids,
    halo_counts,
    halo_dst,
    halo_wt,
    weights,
    cotangent,
):
    row_count, width = features.shape
    layer_count = weights.shape[0]
    parts = lax.axis_size("dom")
    replicas = lax.axis_size("rep")
    slot_count = halo_ids.shape[1]
    capacity = slot_count // parts
    slab = history.shape[1]

    half = layer_count // 2

    wanted = halo_ids.reshape(layer_count, parts, capacity).transpose(1, 0, 2)
    wanted = exchange(wanted.reshape(parts, layer_count * capacity), "dom")
    early = exchange(pull_rows(wanted, history, 0, half, capacity), "dom")
    later = exchange(pull_rows(wanted, history, half, half, capacity), "dom")

    rank = jnp.arange(capacity, dtype=jnp.int32)
    live = rank[None, None, :] < halo_counts[:, :, None]
    wt = jnp.where(live.reshape(layer_count, slot_count), halo_wt.astype(f32), 0.0)
    tiles_t = tiles.transpose(0, 2, 1)

    hidden = features
    supports, slopes, fresh = [], [], []
    for depth in range(half):
        support_bf, slope, hidden = forward_layer(
            depth, depth, tile_cols, hidden, tiles, early, halo_dst, wt, features, weights
        )
        supports.append(support_bf)
        slopes.append(slope)
        fresh.append(hidden)
    near = [send_near(fresh[0]), send_near(hidden)]
    near[0], hidden = lax.optimization_barrier((near[0], hidden))
    far = [send_far(near[0])]
    later, near[1], far[0] = lax.optimization_barrier((later, near[1], far[0]))
    last, grads = finish(
        half, tile_cols, hidden, later, halo_dst, wt, weights,
        tiles, features, cotangent, tiles_t, supports, slopes,
    )
    fresh.append(last[0])
    hidden = last[1]
    near.append(send_near(fresh[2]))
    far.append(send_far(near[1]))
    chunk = layer_count * width // parts
    def own(layer):
        return (layer, 0, 0, fresh[layer])

    def beside(layer):
        return [(layer, replicas - 1, 0, near[layer][0]), (layer, 1, 0, near[layer][1])]

    def across(layer):
        return [(layer, 2, 0, far[layer][0]), (layer, 2, row_count // 2, far[layer][1])]

    place = functools.partial(assemble, layer_count - 1, replicas, row_count)
    mine = exchange(grads.reshape(parts, chunk, width), "dom")
    new_history = place([own(0), own(1), own(2)] + beside(0) + across(0) + beside(1), None)
    mine, near[2], new_history = lax.optimization_barrier((mine, near[2], new_history))
    far.append(send_far(near[2]))
    mine = mine.astype(f32).sum(axis=0)
    mine = exchange(jnp.broadcast_to(mine[None], (replicas, chunk, width)), "rep")
    mine = mine.sum(axis=0)
    whole = exchange(jnp.broadcast_to(mine.astype(bf16)[None], (parts, chunk, width)), "dom")
    weight_grad = whole.astype(f32).reshape(layer_count, width, width)
    new_history = place(beside(2), new_history)
    new_history = place(across(1) + across(2), new_history)
    return (hidden, new_history, weight_grad)


def solution(mesh):
    in_specs = (
        P(("dom", "rep"), None),
        P(None, "dom", None),
        P(("dom", "rep"), None, None),
        P(("dom", "rep")),
        P(None, ("dom", "rep")),
        P(None, ("dom", "rep")),
        P(None, ("dom", "rep")),
        P(None, ("dom", "rep")),
        P(),
        P(("dom", "rep"), None),
    )
    out_specs = (P(("dom", "rep"), None), P(None, "dom", None), P())
    return jax.shard_map(body, mesh=mesh, in_specs=in_specs, out_specs=out_specs, check_vma=False)
```

```python
import functools

import jax
import jax.numpy as jnp
from jax import lax
from jax.experimental import pallas as pl
from jax.experimental.pallas import tpu as pltpu
from jax.sharding import PartitionSpec as P

restart_rate = 0.1
beta_table = [
    0.4054651081081644,
    0.22314355131420976,
    0.15415067982725836,
    0.11778303565638346,
    0.09531017980432493,
    0.08004270767353637,
    0.06899287148695142,
    0.06062462181643484,
]
f32 = jnp.float32
bf16 = jnp.bfloat16
gelu_c = 0.7978845608028654
gelu_k = 0.044715
row_step = 512
vmem_limit = 58 * 1024 * 1024
layer_vmem_limit = 46 * 1024 * 1024
VMEM = pl.BlockSpec(memory_space=pltpu.VMEM)
SMEM = pl.BlockSpec(memory_space=pltpu.SMEM)
ANY = pl.BlockSpec(memory_space=pl.ANY)


def pull_kernel(lo, capacity, wanted, history, rows_o, tables, folded, rows, packed, sems, out_sems):
    count, slab, width = tables.shape
    parts, slots, _ = packed.shape
    lanes = width // 2
    unroll = 4
    cuts = out_sems.shape[0]
    size, share = slab // cuts, parts // cuts
    copies = [
        [
            pltpu.make_async_copy(
                history.at[lo + i, pl.ds(j * size, size), :],
                tables.at[i, pl.ds(j * size, size), :],
                sems.at[i, j],
            )
            for j in range(cuts)
        ]
        for i in range(count)
    ]
    for layer in copies:
        for copy in layer:
            copy.start()
    sent = []
    for layer in range(count):
        for j in range(cuts):
            copies[layer][j].wait()
            for side in range(2):
                folded[pl.ds(2 * j * size + side, size, stride=2), :] = tables[
                    layer, j * size : (j + 1) * size, side * lanes : (side + 1) * lanes
                ].astype(f32)

        def step(i, carry):
            for u in range(unroll):
                part = i * unroll + u
                base = pl.multiple_of(part * (2 * slots), 16)
                for c in range(capacity):
                    row = pl.multiple_of(2 * wanted[part, (lo + layer) * capacity + c], 2)
                    rows[pl.ds(base + 2 * (layer * capacity + c), 2), :] = folded[pl.ds(row, 2), :]
            return carry

        if layer + 1 < count:
            lax.fori_loop(0, parts // unroll, step, 0)
            continue
        for j in range(cuts):
            lax.fori_loop(j * share // unroll, (j + 1) * share // unroll, step, 0)
            for side in range(2):
                half = rows[pl.ds(2 * j * share * slots + side, share * slots, stride=2), :]
                packed[j * share : (j + 1) * share, :, side * lanes : (side + 1) * lanes] = half.reshape(
                    share, slots, lanes
                ).astype(bf16)
            sent.append(
                pltpu.make_async_copy(
                    packed.at[pl.ds(j * share, share)], rows_o.at[pl.ds(j * share, share)], out_sems.at[j]
                )
            )
            sent[j].start()
    for copy in sent:
        copy.wait()


def pull_rows(wanted, history, lo, count, capacity):
    _, slab, width = history.shape
    parts = wanted.shape[0]
    shape = (parts, count * capacity, width)
    cuts = 4
    return pl.pallas_call(
        functools.partial(pull_kernel, lo, capacity),
        out_shape=jax.ShapeDtypeStruct(shape, bf16),
        in_specs=[SMEM, ANY],
        out_specs=ANY,
        scratch_shapes=[
            pltpu.VMEM((count, slab, width), bf16),
            pltpu.VMEM((2 * slab, width // 2), f32),
            pltpu.VMEM((2 * parts * count * capacity, width // 2), f32),
            pltpu.VMEM(shape, bf16),
            pltpu.SemaphoreType.DMA((count, cuts)),
            pltpu.SemaphoreType.DMA((cuts,)),
        ],
        compiler_params=pltpu.CompilerParams(vmem_limit_bytes=vmem_limit),
        cost_estimate=pl.CostEstimate(flops=0, bytes_accessed=20_000_000, transcendentals=0),
    )(wanted, history)


def forward_math(depth, at, cols, hidden, tiles, pulled, dst, wt, features, weights, support_o, slope_o, hidden_o):
    beta = beta_table[depth]
    parts, _, width = pulled.shape
    slots = dst.shape[1]
    capacity = slots // parts
    row_count = features.shape[0]
    step = row_step
    per_block = tiles.shape[0] // (row_count // 128)
    dst_row = dst[depth : depth + 1, :]
    wt_row = wt[depth : depth + 1, :]
    for chunk in range(row_count // step):
        lo = chunk * step
        position = lax.broadcasted_iota(jnp.int32, (step, slots), 0) + lo
        scatter = jnp.where(dst_row == position, wt_row, 0.0).astype(bf16)
        acc = jnp.dot(
            scatter,
            pulled[:, at * capacity : (at + 1) * capacity, :].reshape(slots, width),
            preferred_element_type=f32,
        )
        parts_of = []
        for block in range(lo // 128, (lo + step) // 128):
            picked = jnp.concatenate(
                [
                    hidden[pl.ds(pl.multiple_of(cols[block * per_block + k] * 128, 128), 128), :]
                    for k in range(per_block)
                ],
                axis=0,
            )
            tile_row = jnp.concatenate([tiles[block * per_block + k] for k in range(per_block)], axis=1)
            parts_of.append(jnp.dot(tile_row, picked, preferred_element_type=f32))
        acc = acc + jnp.concatenate(parts_of, axis=0)
        support = (1.0 - restart_rate) * acc + restart_rate * features[lo : lo + step, :].astype(f32)
        support_bf = support.astype(bf16)
        support_o[lo : lo + step, :] = support_bf
        pre = (1.0 - beta) * support + beta * jnp.dot(
            support_bf, weights[depth], preferred_element_type=f32
        )
        square = pre * pre
        th = jnp.tanh(gelu_c * (pre + gelu_k * pre * square))
        half = 0.5 * (1.0 + th)
        hidden_o[lo : lo + step, :] = (pre * half).astype(bf16)
        slope_o[lo : lo + step, :] = half + 0.5 * pre * (1.0 - th * th) * (
            gelu_c * (1.0 + 3.0 * gelu_k * square)
        )


def forward_layer(depth, at, cols, hidden, tiles, pulled, dst, wt, features, weights):
    rows, width = features.shape
    return pl.pallas_call(
        functools.partial(forward_math, depth, at),
        out_shape=(
            jax.ShapeDtypeStruct((rows, width), bf16),
            jax.ShapeDtypeStruct((rows, width), f32),
            jax.ShapeDtypeStruct((rows, width), bf16),
        ),
        in_specs=[SMEM] + [VMEM] * 7,
        out_specs=(VMEM, VMEM, VMEM),
        compiler_params=pltpu.CompilerParams(vmem_limit_bytes=layer_vmem_limit),
        cost_estimate=pl.CostEstimate(flops=1_300_000_000, bytes_accessed=6_000_000, transcendentals=262144),
    )(cols, hidden, tiles, pulled, dst, wt, features, weights)


def finish_kernel(half, *refs):
    cols, hidden, pulled, dst, wt, weights = refs[:6]
    count = 4 + 2 * half
    away, refs = refs[6 : 6 + count], refs[6 + count :]
    fresh, grads_o, refs = refs[:half], refs[half], refs[half + 1 :]
    held, refs = refs[:count], refs[count:]
    supports = held[4 : 4 + half] + refs[:half]
    slopes = held[4 + half :] + refs[half : 2 * half]
    total, grad_bf, gs_bf, sems = refs[2 * half :]
    tiles, features, cot, tiles_t = held[:4]
    copies = [pltpu.make_async_copy(a, b, sems.at[i]) for i, (a, b) in enumerate(zip(away, held))]
    for copy in copies:
        copy.start()
    copies[0].wait()
    copies[1].wait()
    for i in range(half):
        depth = half + i
        forward_math(
            depth, i, cols, hidden, tiles, pulled, dst, wt, features, weights,
            supports[depth], slopes[depth], fresh[i],
        )
        hidden = fresh[i]
    for copy in copies[2:]:
        copy.wait()
    backward_math(cols, cot, tiles_t, weights, supports, slopes, grads_o, total, grad_bf, gs_bf)


def backward_math(cols, cot, tiles_t, weights, supports, slopes, grads_o, total, grad_bf, gs_bf):
    layer_count = weights.shape[0]
    row_count, width = cot.shape
    step = row_step
    per_block = tiles_t.shape[0] // (row_count // 128)
    for depth in range(layer_count - 1, -1, -1):
        beta = beta_table[depth]
        weight = weights[depth]
        for chunk in range(row_count // step):
            lo = chunk * step
            if depth == layer_count - 1:
                grad_out = cot[lo : lo + step, :].astype(f32)
            else:
                grad_out = ((1.0 - restart_rate) * total[lo : lo + step, :]).astype(bf16).astype(f32)
            gp = grad_out * slopes[depth][lo : lo + step, :]
            gp_bf = gp.astype(bf16)
            grad_bf[lo : lo + step, :] = gp_bf
            if depth > 0:
                gs = (1.0 - beta) * gp + beta * lax.dot_general(
                    gp_bf, weight, (((1,), (1,)), ((), ())), preferred_element_type=f32
                )
                gs_bf[lo : lo + step, :] = gs.astype(bf16)
        grads_o[depth] = (
            beta
            * lax.dot_general(
                supports[depth][...], grad_bf[...], (((0,), (0,)), ((), ())), preferred_element_type=f32
            )
        ).astype(bf16)
        if depth > 0:
            total[...] = jnp.zeros_like(total)
            for block in range(row_count // 128):
                tile_col = jnp.concatenate(
                    [tiles_t[block * per_block + k] for k in range(per_block)], axis=0
                )
                product = jnp.dot(
                    tile_col, gs_bf[block * 128 : (block + 1) * 128, :], preferred_element_type=f32
                )
                for k in range(per_block):
                    at = pl.ds(pl.multiple_of(cols[block * per_block + k] * 128, 128), 128)
                    total[at, :] = total[at, :] + product[k * 128 : (k + 1) * 128, :]


def finish(half, cols, hidden, pulled, dst, wt, weights, tiles, features, cot, tiles_t, supports, slopes):
    layer_count, width, _ = weights.shape
    away = [tiles, features, cot, tiles_t, *supports, *slopes]
    block = jax.ShapeDtypeStruct(features.shape, bf16)
    new = layer_count - half
    outs = pl.pallas_call(
        functools.partial(finish_kernel, half),
        out_shape=(block,) * new + (jax.ShapeDtypeStruct((layer_count, width, width), bf16),),
        in_specs=[SMEM] + [VMEM] * 5 + [ANY] * len(away),
        out_specs=(VMEM,) * (new + 1),
        scratch_shapes=[pltpu.VMEM(a.shape, a.dtype) for a in away]
        + [pltpu.VMEM(features.shape, bf16)] * new
        + [pltpu.VMEM(features.shape, f32)] * new
        + [
            pltpu.VMEM(features.shape, f32),
            pltpu.VMEM(features.shape, bf16),
            pltpu.VMEM(features.shape, bf16),
            pltpu.SemaphoreType.DMA((len(away),)),
        ],
        compiler_params=pltpu.CompilerParams(vmem_limit_bytes=vmem_limit),
        cost_estimate=pl.CostEstimate(flops=5_000_000_000, bytes_accessed=12_000_000, transcendentals=524288),
    )(cols, hidden, pulled, dst, wt, weights, *away)
    return outs[:new], outs[new]


def assemble_kernel(places, replicas, rows, count, *refs):
    pieces = refs[:count]
    out, sems = refs[-2:]
    me = lax.axis_index("rep")
    copies = []
    for i, (layer, ahead, offset) in enumerate(places):
        at = lax.rem(me + ahead, replicas) * rows + offset
        size = pieces[i].shape[0]
        copies.append(
            pltpu.make_async_copy(
                pieces[i], out.at[layer, pl.ds(pl.multiple_of(at, 128), size), :], sems.at[i]
            )
        )
    for copy in copies:
        copy.start()
    for copy in copies:
        copy.wait()


def assemble(layers, replicas, rows, pieces, so_far):
    places = [piece[:3] for piece in pieces]
    blocks = [piece[3] for piece in pieces]
    width = blocks[0].shape[1]
    extra = [] if so_far is None else [so_far]
    return pl.pallas_call(
        functools.partial(assemble_kernel, places, replicas, rows, len(blocks)),
        out_shape=jax.ShapeDtypeStruct((layers, replicas * rows, width), bf16),
        in_specs=[VMEM] * len(blocks) + [ANY] * len(extra),
        out_specs=ANY,
        input_output_aliases={len(blocks): 0} if extra else {},
        scratch_shapes=[pltpu.SemaphoreType.DMA((len(blocks),))],
        cost_estimate=pl.CostEstimate(flops=0, bytes_accessed=4_200_000, transcendentals=0),
    )(*blocks, *extra)


def move(value, by):
    size = lax.axis_size("rep")
    return lax.ppermute(value, "rep", [(i, (i + by) % size) for i in range(size)])


def send_near(value):
    return [move(value, 1), move(value, -1)]


def send_far(near):
    half = near[0].shape[0] // 2
    return [move(near[0][:half], 1), move(near[1][half:], -1)]


def exchange(value, axis):
    return lax.all_to_all(value, axis, split_axis=0, concat_axis=0, tiled=True)


def body(
    features,
    history,
    tiles,
    tile_cols,
    halo_ids,
    halo_counts,
    halo_dst,
    halo_wt,
    weights,
    cotangent,
):
    row_count, width = features.shape
    layer_count = weights.shape[0]
    parts = lax.axis_size("dom")
    replicas = lax.axis_size("rep")
    slot_count = halo_ids.shape[1]
    capacity = slot_count // parts
    slab = history.shape[1]

    half = layer_count // 2

    wanted = halo_ids.reshape(layer_count, parts, capacity).transpose(1, 0, 2)
    wanted = exchange(wanted.reshape(parts, layer_count * capacity), "dom")
    early = exchange(pull_rows(wanted, history, 0, half, capacity), "dom")
    later = exchange(pull_rows(wanted, history, half, half, capacity), "dom")

    rank = jnp.arange(capacity, dtype=jnp.int32)
    live = rank[None, None, :] < halo_counts[:, :, None]
    wt = jnp.where(live.reshape(layer_count, slot_count), halo_wt.astype(f32), 0.0)
    tiles_t = tiles.transpose(0, 2, 1)

    hidden = features
    supports, slopes, fresh = [], [], []
    for depth in range(half):
        support_bf, slope, hidden = forward_layer(
            depth, depth, tile_cols, hidden, tiles, early, halo_dst, wt, features, weights
        )
        supports.append(support_bf)
        slopes.append(slope)
        fresh.append(hidden)
    near = [send_near(fresh[0]), send_near(hidden)]
    near[0], hidden = lax.optimization_barrier((near[0], hidden))
    far = [send_far(near[0])]
    later, near[1], far[0] = lax.optimization_barrier((later, near[1], far[0]))
    last, grads = finish(
        half, tile_cols, hidden, later, halo_dst, wt, weights,
        tiles, features, cotangent, tiles_t, supports, slopes,
    )
    fresh.append(last[0])
    hidden = last[1]
    near.append(send_near(fresh[2]))
    far.append(send_far(near[1]))
    chunk = layer_count * width // parts
    def own(layer):
        return (layer, 0, 0, fresh[layer])

    def beside(layer):
        return [(layer, replicas - 1, 0, near[layer][0]), (layer, 1, 0, near[layer][1])]

    def across(layer):
        return [(layer, 2, 0, far[layer][0]), (layer, 2, row_count // 2, far[layer][1])]

    place = functools.partial(assemble, layer_count - 1, replicas, row_count)
    mine = exchange(grads.reshape(parts, chunk, width), "dom")
    new_history = place([own(0), own(1), own(2)] + beside(0) + across(0) + beside(1), None)
    mine, near[2], new_history = lax.optimization_barrier((mine, near[2], new_history))
    far.append(send_far(near[2]))
    mine = mine.astype(f32).sum(axis=0)
    mine = exchange(jnp.broadcast_to(mine[None], (replicas, chunk, width)), "rep")
    mine = mine.sum(axis=0)
    whole = exchange(jnp.broadcast_to(mine.astype(bf16)[None], (parts, chunk, width)), "dom")
    weight_grad = whole.astype(f32).reshape(layer_count, width, width)
    new_history = place(beside(2), new_history)
    new_history = place(across(1), new_history)
    new_history = place(across(2), new_history)
    return (hidden, new_history, weight_grad)


def solution(mesh):
    in_specs = (
        P(("dom", "rep"), None),
        P(None, "dom", None),
        P(("dom", "rep"), None, None),
        P(("dom", "rep")),
        P(None, ("dom", "rep")),
        P(None, ("dom", "rep")),
        P(None, ("dom", "rep")),
        P(None, ("dom", "rep")),
        P(),
        P(("dom", "rep"), None),
    )
    out_specs = (P(("dom", "rep"), None), P(None, "dom", None), P())
    return jax.shard_map(body, mesh=mesh, in_specs=in_specs, out_specs=out_specs, check_vma=False)
```
